32 devices in a mesh: grp: 4 (over z), dom: 2 (over y), rel: 4 (over x, core).
Axes of the slice: x: 2, y: 2, z: 4, core: 2. Of those that a mesh axis runs over, the one named last changes fastest.
Arguments:
- features: bfloat16 [8192, 768], P(('grp', 'dom', 'rel')), may hold values from -6 to 6
- send_list: int32 [32, 2, 1], P(('grp', 'dom', 'rel')), may hold values from 0 to 1
- tile_values: bfloat16 [32, 2, 4, 128, 128], P(('grp', 'dom', 'rel')), may hold values from -0.1875 to 0.1875
- tile_meta: int32 [32, 2, 4, 4], P(('grp', 'dom', 'rel')), may hold values from 0 to 4, as said below
- rel_weight: bfloat16 [5, 768, 1024], replicated, may hold values from -0.21875 to 0.21875
- self_weight: bfloat16 [768, 1024], replicated, may hold values from -0.21875 to 0.21875
- bn_gain: float32 [1024], replicated, may hold values from 0.25 to 1.75
- bn_shift: float32 [1024], replicated, may hold values from -3 to 3
Outputs:
- activated: bfloat16 [8192, 1024], P(('grp', 'dom', 'rel'))
The draws below stay inside these ranges and needn't reach their ends.
Inputs may be any that keep to these rules, and one draw needn't show every extreme that they name: `tile_meta`: entry [p, d, r] describes the tile that partition p holds for the partition of its group with dom index d and rel index r: relation below 5, destination block below 2, source table entry below 4, live flag 0 or 1. The live tiles received by one partition have distinct (relation, destination, source); in every group some partition receives only live tiles.
All inputs are finite; a program needn't handle non-finite values.
Results may differ from the reference program's by a relative error of at most 0.003.
Values may be sent and summed in bfloat16 or wider, within the bound.
A program may use at most 128 MiB of HBM per device.

```python
import jax
import jax.numpy as jnp
from jax import lax

F = 768
HID = 1024
REL = 5
BLK = 128
FS = 1
NB_DEV = 2
NPART = 32
NODES = 8192
N_GRP = 4
N_DOM = 2
N_REL = 4


def draw_tile_meta(key, part):
    key = jax.random.fold_in(key, 11)
    groups, doms, rels = (N_GRP, N_DOM, N_REL)
    parts = groups * doms * rels
    slots = doms * rels
    table_size = NB_DEV + doms * FS
    combos = REL * NB_DEV * table_size
    keys = jax.random.split(key, 3)
    perm_keys = jax.random.split(keys[0], parts)
    picks = jax.vmap(lambda single: jax.random.permutation(single, combos)[:slots])(perm_keys)
    picks = picks.astype(jnp.int32)
    relation = picks // (NB_DEV * table_size)
    target = picks // table_size % NB_DEV
    source = picks % table_size
    level = jax.random.randint(keys[1], (parts, 1), 1, 5)
    position = jnp.arange(parts, dtype=jnp.int32)[:, None]
    level = jnp.where(position % slots == 0, 4, level)
    coin = jax.random.randint(keys[2], (parts, slots), 0, 4)
    live = (coin < level).astype(jnp.int32)
    meta = jnp.stack([relation, target, source, live], axis=-1).astype(jnp.int32)
    meta = meta.reshape(groups, doms, rels, doms, rels, 4)
    meta = jnp.transpose(meta, (0, 3, 4, 1, 2, 5))
    return meta.reshape(parts, doms, rels, 4)


def set_ends(values, key, low, largest):
    longest = values.shape.index(max(values.shape))
    spots = []
    for shift in (0, 1):
        where = [jax.random.randint(jax.random.fold_in(key, axis), (), 0, length) for axis, length in enumerate(values.shape)]
        where[longest] = (where[longest] + shift) % values.shape[longest]
        spots.append(tuple(where))
    return values.at[spots[0]].set(low).at[spots[1]].set(largest)


def shard_levels(key, shape, shards, low, top_value):
    level = 1.0
    for dim, blocks in shards:
        steps = jax.random.uniform(jax.random.fold_in(jax.random.fold_in(key, 6), dim), (blocks,), jnp.float32, low / len(shards), top_value / len(shards))
        level = level * jnp.repeat(jnp.exp(steps), shape[dim] // blocks).reshape((-1,) + (1,) * (len(shape) - 1 - dim))
    return level


def bell_draw(stream_key, dims, width, reach, pieces=(), kind=jnp.bfloat16):
    array = jax.random.normal(stream_key, dims, jnp.float32) * width
    if len(pieces) > 0:
        array = shard_levels(stream_key, dims, pieces, -0.22, 0.18) * array
    return jnp.clip(array, min=-reach, max=reach).astype(kind)


def setup_inputs(seed: int = 0) -> dict:
    key_list = jax.random.split(jax.random.key(seed), 9)
    return {
        "features": bell_draw(key_list[0], (NODES, F), 1.0, 6.0, ((0, 32),)),
        "send_list": set_ends(jax.random.randint(key_list[1], (NPART, N_DOM, FS), 0, NB_DEV), jax.random.fold_in(key_list[1], 1), 0, NB_DEV - 1).astype(jnp.int32),
        "tile_values": bell_draw(key_list[2], (NPART, N_DOM, N_REL, BLK, BLK), (BLK * N_DOM * N_REL) ** -0.5, 0.1875, ((0, 32),)),
        "tile_meta": draw_tile_meta(jax.random.fold_in(key_list[8], 71), 0),
        "rel_weight": bell_draw(key_list[4], (REL, F, HID), F ** -0.5, 0.21875),
        "self_weight": bell_draw(key_list[5], (F, HID), F ** -0.5, 0.21875),
        "bn_gain": jnp.clip(1.0 + 0.15 * jax.random.normal(key_list[6], (HID,), jnp.float32), 0.25, 1.75),
        "bn_shift": bell_draw(key_list[7], (HID,), 0.5, 3.0, (), jnp.float32),
    }


def reference(features, send_list, tile_values, tile_meta, rel_weight, self_weight, bn_gain, bn_shift):
    groups, doms, rels = (N_GRP, N_DOM, N_REL)
    parts = groups * doms * rels
    blocks = features.reshape(groups, doms, rels, NB_DEV, BLK, F)
    lists = send_list.reshape(groups, doms, rels, doms, FS)
    tiles = tile_values.reshape(groups, doms, rels, doms, rels, BLK, BLK)
    metas = tile_meta.reshape(groups, doms, rels, doms, rels, 4)

    def one_part(index):
        group = index // (doms * rels)
        dom_at = index // rels % doms
        rel_at = index % rels
        own = blocks[group, dom_at, rel_at]
        senders = blocks[group, :, rel_at]
        picks = lists[group, :, rel_at, dom_at, :]
        rows = jnp.arange(doms, dtype=jnp.int32)[:, None]
        received = senders[rows, picks].reshape(doms * FS, BLK, F)
        table = jnp.concatenate([own, received], axis=0)
        values = tiles[group, :, :, dom_at, rel_at].reshape(doms * rels, BLK, BLK)
        meta = metas[group, :, :, dom_at, rel_at].reshape(doms * rels, 4)
        sources = table[meta[:, 2]]
        message = jnp.einsum('kij,kjf->kif', values.astype(jnp.float32), sources.astype(jnp.float32))
        code = meta[:, 0] * NB_DEV + meta[:, 1]
        slots = jnp.arange(REL * NB_DEV, dtype=jnp.int32)
        select = (code[:, None] == slots[None, :]).astype(jnp.float32) * meta[:, 3:4].astype(jnp.float32)
        summed = jnp.einsum('kc,kif->cif', select, message, precision=lax.Precision.HIGHEST)
        return summed.astype(jnp.bfloat16)
    aggregated = lax.map(one_part, jnp.arange(parts, dtype=jnp.int32))
    aggregated = aggregated.reshape(parts, REL, NB_DEV * BLK, F)
    pre = jnp.dot(features, self_weight, preferred_element_type=jnp.float32)
    for kind in range(REL):
        rows_kind = aggregated[:, kind].reshape(parts * NB_DEV * BLK, F)
        pre = pre + jnp.dot(rows_kind, rel_weight[kind], preferred_element_type=jnp.float32)
    mean = lax.optimization_barrier(jnp.mean(pre, axis=0))
    centered = pre - mean
    variance = lax.optimization_barrier(jnp.mean(centered * centered, axis=0))
    normed = centered / jnp.sqrt(variance + 1e-05) * bn_gain + bn_shift
    return jax.nn.elu(normed).astype(jnp.bfloat16)
```

```python
import functools

import jax
import jax.numpy as jnp
from jax import lax
from jax.experimental import pallas as pl
from jax.experimental.pallas import tpu as pltpu
from jax.sharding import PartitionSpec as P

MESH = pl.DeviceIdType.MESH
CODE_ROWS = 16
F_CHUNK = 256
COL_PARTS = 2


def repeat(count, body, static):
    if static:
        for index in range(count):
            body(index)
    else:

        @pl.loop(0, count)
        def _(index):
            body(index)


def aligned(index, size):
    return pl.ds(pl.multiple_of(index * size, size), size)


def kernel(
    groups,
    doms,
    rels,
    features,
    send_list,
    tile_values,
    tile_meta,
    rel_weight,
    self_weight,
    bn_gain,
    bn_shift,
    out,
    table,
    picked,
    message_out,
    message_in,
    adjacency,
    aggregated,
    weights,
    root,
    pre,
    group_stats,
    all_stats,
    result,
    own,
    own_sem,
    feature_sem,
    tile_sem,
    weight_sem,
    root_sem,
    message_send,
    message_recv,
    block_send,
    block_recv,
    group_send,
    group_recv,
    all_send,
    all_recv,
    out_sem,
):
    rows, width = features.shape
    kinds, _, hidden = rel_weight.shape
    block = tile_values.shape[-1]
    nblocks = rows // block
    slots = doms * rels
    sources = nblocks + doms
    chunks = width // F_CHUNK
    columns = hidden // COL_PARTS
    static = slots <= 16
    my_grp = lax.axis_index("grp")
    my_dom = lax.axis_index("dom")
    my_rel = lax.axis_index("rel")
    me = my_dom * rels + my_rel

    def peer(offset):
        target = lax.rem(me + offset, slots)
        return target // rels, lax.rem(target, rels)

    def group_peer(offset):
        dom, rel = peer(offset)
        return {"dom": dom, "rel": rel}

    def far_peer(offset):
        return {"grp": lax.rem(my_grp + offset, groups)}

    def tile_copy(offset):
        dom, rel = peer(offset)
        return pltpu.make_async_copy(
            tile_values.at[0, dom, rel],
            message_out.at[offset, pl.ds(0, block)],
            tile_sem.at[offset],
        )

    own_tile = pltpu.make_async_copy(
        tile_values.at[0, my_dom, my_rel], message_in.at[0, pl.ds(0, block)], tile_sem.at[0]
    )
    own_features = pltpu.make_async_copy(features, table.at[pl.ds(0, rows)], feature_sem)

    own_copy = pltpu.make_async_copy(features, own, own_sem)
    own_copy.start()
    own_features.start()
    repeat(slots - 1, lambda i: tile_copy(i + 1).start(), static)
    own_tile.start()

    barrier = pltpu.get_barrier_semaphore()

    def greet_group(i):
        pl.semaphore_signal(barrier, inc=1, device_id=group_peer(i + 1), device_id_type=MESH)

    def greet_far(i):
        pl.semaphore_signal(barrier, inc=1, device_id=far_peer(i + 1), device_id_type=MESH)

    repeat(slots - 1, greet_group, static)
    repeat(groups - 1, greet_far, static)

    root_copy = pltpu.make_async_copy(self_weight, root, root_sem)
    root_copy.start()

    def weight_copy(chunk, kind):
        return pltpu.make_async_copy(
            rel_weight.at[kind, pl.ds(chunk * F_CHUNK, F_CHUNK)],
            weights.at[chunk, pl.ds(kind * F_CHUNK, F_CHUNK)],
            weight_sem.at[chunk, kind],
        )

    for chunk in range(chunks):
        for kind in range(kinds):
            weight_copy(chunk, kind).start()

    def write_code(offset, ref):
        dom, rel = peer(offset)
        source = tile_meta[0, dom, rel, 2]
        around = dom - (source - nblocks)
        around = jnp.where(around < 0, around + doms, around)
        place = jnp.where(source < nblocks, source, nblocks + around)
        row = tile_meta[0, dom, rel, 0] * nblocks + tile_meta[0, dom, rel, 1]
        code = jnp.where(tile_meta[0, dom, rel, 3] != 0, row * sources + place, -1)
        splat = jnp.full((CODE_ROWS, block), code.astype(jnp.float32), jnp.float32)
        ref[offset, pl.ds(block, CODE_ROWS), :] = splat.astype(jnp.bfloat16)

    write_code(0, message_in)
    repeat(slots - 1, lambda i: write_code(i + 1, message_out), static)

    own_copy.wait()

    def pick(offset):
        chosen = send_list[0, lax.rem(my_dom + offset, doms), 0]
        chosen = jnp.full((block, width), chosen.astype(jnp.float32)).astype(jnp.bfloat16)
        total = own[pl.ds(0, block), :]
        for index in range(1, nblocks):
            here = own[pl.ds(index * block, block), :]
            total = jnp.where(chosen == jnp.bfloat16(index), here, total)
        return total

    for offset in range(1, doms):
        picked[offset - 1] = pick(offset)
    table[pl.ds(nblocks * block, block), :] = pick(0)

    pl.semaphore_wait(barrier, slots - 1 + groups - 1)

    def message_copy(offset):
        return pltpu.make_async_remote_copy(
            src_ref=message_out.at[offset],
            dst_ref=message_in.at[offset],
            send_sem=message_send.at[offset],
            recv_sem=message_recv.at[offset],
            device_id=group_peer(offset),
            device_id_type=MESH,
        )

    def send_message(i):
        tile_copy(i + 1).wait()
        message_copy(i + 1).start()

    repeat(slots - 1, send_message, static)

    def block_copy(offset, chunk):
        part = pl.ds(chunk * F_CHUNK, F_CHUNK)
        return pltpu.make_async_remote_copy(
            src_ref=picked.at[offset - 1, :, part],
            dst_ref=table.at[pl.ds((nblocks + offset) * block, block), part],
            send_sem=block_send.at[chunk, offset - 1],
            recv_sem=block_recv.at[chunk, offset - 1],
            device_id={"dom": lax.rem(my_dom + offset, doms)},
            device_id_type=MESH,
        )

    for chunk in range(chunks):
        for offset in range(1, doms):
            block_copy(offset, chunk).start()

    root_copy.wait()
    own_features.wait()
    pre[...] = jnp.dot(own[...], root[...], preferred_element_type=jnp.float32)

    own_tile.wait()
    repeat(slots - 1, lambda i: message_copy(i + 1).wait_recv(), static)

    zero = jnp.zeros((CODE_ROWS, block), jnp.bfloat16)

    def place_tile(row, source, strip):
        code = row * sources + source
        if static:
            total = zero
            wanted = jnp.bfloat16(code)
            for slot in range(slots):
                same = message_in[slot, pl.ds(block, CODE_ROWS), :] == wanted
                total = jnp.where(
                    same, message_in[slot, aligned(strip, CODE_ROWS), :], total
                )
        else:
            wanted = jnp.full((CODE_ROWS, block), code.astype(jnp.float32)).astype(jnp.bfloat16)

            def step(slot, total):
                same = message_in[slot, pl.ds(block, CODE_ROWS), :] == wanted
                return jnp.where(
                    same, message_in[slot, aligned(strip, CODE_ROWS), :], total
                )

            total = lax.fori_loop(0, slots, step, zero)
        first = pl.multiple_of(row * block + strip * CODE_ROWS, CODE_ROWS)
        adjacency[pl.ds(first, CODE_ROWS), aligned(source, block)] = total

    @pl.loop(0, block // CODE_ROWS)
    def _(strip):
        repeat(
            kinds * nblocks,
            lambda row: repeat(sources, lambda source: place_tile(row, source, strip), static),
            static,
        )

    def aggregate(chunk):
        for offset in range(1, doms):
            block_copy(offset, chunk).wait_recv()
        part = pl.ds(chunk * F_CHUNK, F_CHUNK)
        for kind in range(kinds):
            weight_copy(chunk, kind).wait()
        for kind in range(kinds):
            aggregated[:, pl.ds(kind * F_CHUNK, F_CHUNK)] = jnp.dot(
                adjacency[pl.ds(kind * rows, rows), :],
                table[:, part],
                preferred_element_type=jnp.float32,
            ).astype(jnp.bfloat16)

    for chunk in range(chunks - 1):
        aggregate(chunk)
        pre[...] += jnp.dot(
            aggregated[...], weights[chunk], preferred_element_type=jnp.float32
        )

    aggregate(chunks - 1)

    def group_copy(part, offset):
        return pltpu.make_async_remote_copy(
            src_ref=group_stats.at[part, 0],
            dst_ref=group_stats.at[part, offset],
            send_sem=group_send.at[part, offset],
            recv_sem=group_recv.at[part, offset],
            device_id=group_peer(offset),
            device_id_type=MESH,
        )

    def far_copy(part, offset):
        return pltpu.make_async_remote_copy(
            src_ref=all_stats.at[part, 0],
            dst_ref=all_stats.at[part, offset],
            send_sem=all_send.at[part, offset],
            recv_sem=all_recv.at[part, offset],
            device_id=far_peer(offset),
            device_id_type=MESH,
        )

    def combine(stats, part, count, each):
        entries = [stats[part, index] for index in range(count)]
        mean = sum(entry[0:1] for entry in entries) * (1.0 / count)
        spread = sum(entry[1:2] for entry in entries)
        apart = [entry[0:1] - mean for entry in entries]
        return mean, spread + sum(gap * gap for gap in apart) * each

    for part in range(COL_PARTS):
        span = pl.ds(part * columns, columns)
        value = pre[:, span] + jnp.dot(
            aggregated[...], weights[chunks - 1, :, span], preferred_element_type=jnp.float32
        )
        pre[:, span] = value
        mean = jnp.sum(value, axis=0, keepdims=True) * (1.0 / rows)
        centered = value - mean
        group_stats[part, 0, 0:1, :] = mean
        group_stats[part, 0, 1:2, :] = jnp.sum(centered * centered, axis=0, keepdims=True)
        repeat(slots - 1, lambda i: group_copy(part, i + 1).start(), static)

    for part in range(COL_PARTS):
        repeat(slots - 1, lambda i: group_copy(part, i + 1).wait_recv(), static)
        mean, spread = combine(group_stats, part, slots, float(rows))
        all_stats[part, 0, 0:1, :] = mean
        all_stats[part, 0, 1:2, :] = spread
        repeat(groups - 1, lambda i: far_copy(part, i + 1).start(), static)

    copies = []
    for part in range(COL_PARTS):
        span = pl.ds(part * columns, columns)
        repeat(groups - 1, lambda i: far_copy(part, i + 1).wait_recv(), static)
        mean, spread = combine(all_stats, part, groups, float(rows * slots))
        variance = spread * (1.0 / (rows * slots * groups))
        scale = bn_gain[:, span] / jnp.sqrt(variance + 1e-05)
        normed = (pre[:, span] - mean) * scale + bn_shift[:, span]
        below = jnp.exp(jnp.minimum(normed, 0.0)) - 1.0
        result[:, span] = jnp.where(normed > 0, normed, below).astype(jnp.bfloat16)
        copy = pltpu.make_async_copy(result.at[:, span], out.at[:, span], out_sem.at[part])
        copy.start()
        copies.append(copy)

    repeat(slots - 1, lambda i: message_copy(i + 1).wait_send(), static)
    for chunk in range(chunks):
        for offset in range(1, doms):
            block_copy(offset, chunk).wait_send()
    for part in range(COL_PARTS):
        repeat(slots - 1, lambda i: group_copy(part, i + 1).wait_send(), static)
        repeat(groups - 1, lambda i: far_copy(part, i + 1).wait_send(), static)
    for copy in copies:
        copy.wait()


def body(features, send_list, tile_values, tile_meta, rel_weight, self_weight, bn_gain, bn_shift):
    rows, width = features.shape
    kinds, _, hidden = rel_weight.shape
    block = tile_values.shape[-1]
    nblocks = rows // block
    groups = lax.axis_size("grp")
    doms = lax.axis_size("dom")
    rels = lax.axis_size("rel")
    slots = doms * rels
    sources = nblocks + doms
    chunks = width // F_CHUNK
    columns = hidden // COL_PARTS
    anywhere = pl.BlockSpec(memory_space=pl.ANY)
    scalars = pl.BlockSpec(memory_space=pltpu.SMEM)
    local = pl.BlockSpec(memory_space=pltpu.VMEM)
    dma = pltpu.SemaphoreType.DMA
    return pl.pallas_call(
        functools.partial(kernel, groups, doms, rels),
        out_shape=jax.ShapeDtypeStruct((rows, hidden), jnp.bfloat16),
        in_specs=[anywhere, scalars, anywhere, scalars, anywhere, anywhere, local, local],
        out_specs=anywhere,
        scratch_shapes=[
            pltpu.VMEM((sources * block, width), jnp.bfloat16),
            pltpu.VMEM((doms - 1, block, width), jnp.bfloat16),
            pltpu.VMEM((slots, block + CODE_ROWS, block), jnp.bfloat16),
            pltpu.VMEM((slots, block + CODE_ROWS, block), jnp.bfloat16),
            pltpu.VMEM((kinds * rows, sources * block), jnp.bfloat16),
            pltpu.VMEM((rows, kinds * F_CHUNK), jnp.bfloat16),
            pltpu.VMEM((chunks, kinds * F_CHUNK, hidden), jnp.bfloat16),
            pltpu.VMEM((width, hidden), jnp.bfloat16),
            pltpu.VMEM((rows, hidden), jnp.float32),
            pltpu.VMEM((COL_PARTS, slots, 2, columns), jnp.float32),
            pltpu.VMEM((COL_PARTS, groups, 2, columns), jnp.float32),
            pltpu.VMEM((rows, hidden), jnp.bfloat16),
            pltpu.VMEM((rows, width), jnp.bfloat16),
            dma(()),
            dma(()),
            dma((slots,)),
            dma((chunks, kinds)),
            dma(()),
            dma((slots,)),
            dma((slots,)),
            dma((chunks, doms - 1)),
            dma((chunks, doms - 1)),
            dma((COL_PARTS, slots)),
            dma((COL_PARTS, slots)),
            dma((COL_PARTS, groups)),
            dma((COL_PARTS, groups)),
            dma((COL_PARTS,)),
        ],
        compiler_params=pltpu.CompilerParams(
            collective_id=0, has_side_effects=True, vmem_limit_bytes=48 * 1024 * 1024
        ),
        cost_estimate=pl.CostEstimate(
            flops=2 * rows * (kinds + 1) * width * hidden,
            bytes_accessed=2 * (kinds + 1) * width * hidden,
            transcendentals=rows * hidden,
        ),
    )(
        features,
        send_list,
        tile_values,
        tile_meta,
        rel_weight,
        self_weight,
        bn_gain.reshape(1, hidden),
        bn_shift.reshape(1, hidden),
    )


def solution(mesh):
    return jax.shard_map(
        body,
        mesh=mesh,
        in_specs=(
            P(("grp", "dom", "rel"), None),
            P(("grp", "dom", "rel"), None, None),
            P(("grp", "dom", "rel"), None, None, None, None),
            P(("grp", "dom", "rel"), None, None, None),
            P(),
            P(),
            P(),
            P(),
        ),
        out_specs=P(("grp", "dom", "rel"), None),
        check_vma=False,
    )
```

```python
import functools

import jax
import jax.numpy as jnp
from jax import lax
from jax.experimental import pallas as pl
from jax.experimental.pallas import tpu as pltpu
from jax.sharding import PartitionSpec as P

MESH = pl.DeviceIdType.MESH
CODE_ROWS = 16
F_CHUNK = 256
COL_PARTS = 1


def repeat(count, body, static):
    if static:
        for index in range(count):
            body(index)
    else:

        @pl.loop(0, count)
        def _(index):
            body(index)


def aligned(index, size):
    return pl.ds(pl.multiple_of(index * size, size), size)


def kernel(
    groups,
    doms,
    rels,
    features,
    send_list_hbm,
    tile_values,
    tile_meta_hbm,
    rel_weight,
    self_weight,
    bn_gain_hbm,
    bn_shift_hbm,
    result,
    send_list,
    tile_meta,
    bn_gain,
    bn_shift,
    table,
    picked,
    message_out,
    message_in,
    adjacency,
    aggregated,
    weights,
    root,
    pre,
    group_stats,
    all_stats,
    own,
    small_sem,
    own_sem,
    feature_sem,
    tile_sem,
    weight_sem,
    root_sem,
    message_send,
    message_recv,
    block_send,
    block_recv,
    group_send,
    group_recv,
    all_send,
    all_recv,
):
    rows, width = features.shape
    kinds, _, hidden = rel_weight.shape
    block = tile_values.shape[-1]
    nblocks = rows // block
    slots = doms * rels
    sources = nblocks + doms
    chunks = width // F_CHUNK
    columns = hidden // COL_PARTS
    static = slots <= 16
    my_grp = lax.axis_index("grp")
    my_dom = lax.axis_index("dom")
    my_rel = lax.axis_index("rel")
    me = my_dom * rels + my_rel

    def peer(offset):
        target = lax.rem(me + offset, slots)
        return target // rels, lax.rem(target, rels)

    def group_peer(offset):
        dom, rel = peer(offset)
        return {"dom": dom, "rel": rel}

    def far_peer(offset):
        return {"grp": lax.rem(my_grp + offset, groups)}

    def tile_copy(offset):
        dom, rel = peer(offset)
        return pltpu.make_async_copy(
            tile_values.at[0, dom, rel],
            message_out.at[offset, pl.ds(0, block)],
            tile_sem.at[offset],
        )

    own_tile = pltpu.make_async_copy(
        tile_values.at[0, my_dom, my_rel], message_in.at[0, pl.ds(0, block)], tile_sem.at[0]
    )
    own_features = pltpu.make_async_copy(features, table.at[pl.ds(0, rows)], feature_sem)

    small_copies = [
        pltpu.make_async_copy(source, target, small_sem.at[index])
        for index, (source, target) in enumerate(
            (
                (send_list_hbm, send_list),
                (tile_meta_hbm, tile_meta),
                (bn_gain_hbm, bn_gain),
                (bn_shift_hbm, bn_shift),
            )
        )
    ]
    for copy in small_copies:
        copy.start()
    own_copy = pltpu.make_async_copy(features, own, own_sem)
    own_copy.start()
    own_features.start()
    repeat(slots - 1, lambda i: tile_copy(i + 1).start(), static)
    own_tile.start()

    barrier = pltpu.get_barrier_semaphore()

    def greet_group(i):
        pl.semaphore_signal(barrier, inc=1, device_id=group_peer(i + 1), device_id_type=MESH)

    def greet_far(i):
        pl.semaphore_signal(barrier, inc=1, device_id=far_peer(i + 1), device_id_type=MESH)

    repeat(slots - 1, greet_group, static)
    repeat(groups - 1, greet_far, static)

    root_copy = pltpu.make_async_copy(self_weight, root, root_sem)
    root_copy.start()

    def weight_copy(chunk, kind):
        return pltpu.make_async_copy(
            rel_weight.at[kind, pl.ds(chunk * F_CHUNK, F_CHUNK)],
            weights.at[chunk, pl.ds(kind * F_CHUNK, F_CHUNK)],
            weight_sem.at[chunk, kind],
        )

    for chunk in range(chunks):
        for kind in range(kinds):
            weight_copy(chunk, kind).start()

    def write_code(offset, ref):
        dom, rel = peer(offset)
        source = tile_meta[0, dom, rel, 2]
        around = dom - (source - nblocks)
        around = jnp.where(around < 0, around + doms, around)
        place = jnp.where(source < nblocks, source, nblocks + around)
        row = tile_meta[0, dom, rel, 0] * nblocks + tile_meta[0, dom, rel, 1]
        code = jnp.where(tile_meta[0, dom, rel, 3] != 0, row * sources + place, -1)
        splat = jnp.full((CODE_ROWS, block), code.astype(jnp.float32), jnp.float32)
        ref[offset, pl.ds(block, CODE_ROWS), :] = splat.astype(jnp.bfloat16)

    for copy in small_copies:
        copy.wait()
    write_code(0, message_in)
    repeat(slots - 1, lambda i: write_code(i + 1, message_out), static)

    own_copy.wait()

    def pick(offset):
        chosen = send_list[0, lax.rem(my_dom + offset, doms)]
        chosen = jnp.full((block, width), chosen.astype(jnp.float32)).astype(jnp.bfloat16)
        total = own[pl.ds(0, block), :]
        for index in range(1, nblocks):
            here = own[pl.ds(index * block, block), :]
            total = jnp.where(chosen == jnp.bfloat16(index), here, total)
        return total

    for offset in range(1, doms):
        picked[offset - 1] = pick(offset)
    table[pl.ds(nblocks * block, block), :] = pick(0)

    pl.semaphore_wait(barrier, slots - 1 + groups - 1)

    def message_copy(offset):
        return pltpu.make_async_remote_copy(
            src_ref=message_out.at[offset],
            dst_ref=message_in.at[offset],
            send_sem=message_send.at[offset],
            recv_sem=message_recv.at[offset],
            device_id=group_peer(offset),
            device_id_type=MESH,
        )

    def send_message(i):
        tile_copy(i + 1).wait()
        message_copy(i + 1).start()

    repeat(slots - 1, send_message, static)

    def block_copy(offset, chunk):
        part = pl.ds(chunk * F_CHUNK, F_CHUNK)
        return pltpu.make_async_remote_copy(
            src_ref=picked.at[offset - 1, :, part],
            dst_ref=table.at[pl.ds((nblocks + offset) * block, block), part],
            send_sem=block_send.at[chunk, offset - 1],
            recv_sem=block_recv.at[chunk, offset - 1],
            device_id={"dom": lax.rem(my_dom + offset, doms)},
            device_id_type=MESH,
        )

    for chunk in range(chunks):
        for offset in range(1, doms):
            block_copy(offset, chunk).start()

    root_copy.wait()
    own_features.wait()
    pre[...] = jnp.dot(own[...], root[...], preferred_element_type=jnp.float32)

    own_tile.wait()
    repeat(slots - 1, lambda i: message_copy(i + 1).wait_recv(), static)

    zero = jnp.zeros((CODE_ROWS, block), jnp.bfloat16)

    def place_tile(row, source, strip):
        code = row * sources + source
        if static:
            total = zero
            wanted = jnp.bfloat16(code)
            for slot in range(slots):
                same = message_in[slot, pl.ds(block, CODE_ROWS), :] == wanted
                total = jnp.where(
                    same, message_in[slot, aligned(strip, CODE_ROWS), :], total
                )
        else:
            wanted = jnp.full((CODE_ROWS, block), code.astype(jnp.float32)).astype(jnp.bfloat16)

            def step(slot, total):
                same = message_in[slot, pl.ds(block, CODE_ROWS), :] == wanted
                return jnp.where(
                    same, message_in[slot, aligned(strip, CODE_ROWS), :], total
                )

            total = lax.fori_loop(0, slots, step, zero)
        first = pl.multiple_of(row * block + strip * CODE_ROWS, CODE_ROWS)
        adjacency[pl.ds(first, CODE_ROWS), aligned(source, block)] = total

    @pl.loop(0, block // CODE_ROWS)
    def _(strip):
        repeat(
            kinds * nblocks,
            lambda row: repeat(sources, lambda source: place_tile(row, source, strip), static),
            static,
        )

    def aggregate(chunk):
        for offset in range(1, doms):
            block_copy(offset, chunk).wait_recv()
        part = pl.ds(chunk * F_CHUNK, F_CHUNK)
        for kind in range(kinds):
            weight_copy(chunk, kind).wait()
        for kind in range(kinds):
            aggregated[:, pl.ds(kind * F_CHUNK, F_CHUNK)] = jnp.dot(
                adjacency[pl.ds(kind * rows, rows), :],
                table[:, part],
                preferred_element_type=jnp.float32,
            ).astype(jnp.bfloat16)

    for chunk in range(chunks - 1):
        aggregate(chunk)
        pre[...] += jnp.dot(
            aggregated[...], weights[chunk], preferred_element_type=jnp.float32
        )

    aggregate(chunks - 1)

    def group_copy(part, offset):
        return pltpu.make_async_remote_copy(
            src_ref=group_stats.at[part, 0],
            dst_ref=group_stats.at[part, offset],
            send_sem=group_send.at[part, offset],
            recv_sem=group_recv.at[part, offset],
            device_id=group_peer(offset),
            device_id_type=MESH,
        )

    def far_copy(part, offset):
        return pltpu.make_async_remote_copy(
            src_ref=all_stats.at[part, 0],
            dst_ref=all_stats.at[part, offset],
            send_sem=all_send.at[part, offset],
            recv_sem=all_recv.at[part, offset],
            device_id=far_peer(offset),
            device_id_type=MESH,
        )

    def combine(stats, part, count, each):
        entries = [stats[part, index] for index in range(count)]
        mean = sum(entry[0:1] for entry in entries) * (1.0 / count)
        spread = sum(entry[1:2] for entry in entries)
        apart = [entry[0:1] - mean for entry in entries]
        return mean, spread + sum(gap * gap for gap in apart) * each

    for part in range(COL_PARTS):
        span = pl.ds(part * columns, columns)
        value = pre[:, span] + jnp.dot(
            aggregated[...], weights[chunks - 1, :, span], preferred_element_type=jnp.float32
        )
        pre[:, span] = value
        mean = jnp.sum(value, axis=0, keepdims=True) * (1.0 / rows)
        centered = value - mean
        group_stats[part, 0, 0:1, :] = mean
        group_stats[part, 0, 1:2, :] = jnp.sum(centered * centered, axis=0, keepdims=True)
        repeat(slots - 1, lambda i: group_copy(part, i + 1).start(), static)

    for part in range(COL_PARTS):
        repeat(slots - 1, lambda i: group_copy(part, i + 1).wait_recv(), static)
        mean, spread = combine(group_stats, part, slots, float(rows))
        all_stats[part, 0, 0:1, :] = mean
        all_stats[part, 0, 1:2, :] = spread
        repeat(groups - 1, lambda i: far_copy(part, i + 1).start(), static)

    for part in range(COL_PARTS):
        span = pl.ds(part * columns, columns)
        repeat(groups - 1, lambda i: far_copy(part, i + 1).wait_recv(), static)
        mean, spread = combine(all_stats, part, groups, float(rows * slots))
        variance = spread * (1.0 / (rows * slots * groups))
        scale = bn_gain[:, span] / jnp.sqrt(variance + 1e-05)
        normed = (pre[:, span] - mean) * scale + bn_shift[:, span]
        below = jnp.exp(jnp.minimum(normed, 0.0)) - 1.0
        result[:, span] = jnp.where(normed > 0, normed, below).astype(jnp.bfloat16)

    repeat(slots - 1, lambda i: message_copy(i + 1).wait_send(), static)
    for chunk in range(chunks):
        for offset in range(1, doms):
            block_copy(offset, chunk).wait_send()
    for part in range(COL_PARTS):
        repeat(slots - 1, lambda i: group_copy(part, i + 1).wait_send(), static)
        repeat(groups - 1, lambda i: far_copy(part, i + 1).wait_send(), static)


def body(features, send_list, tile_values, tile_meta, rel_weight, self_weight, bn_gain, bn_shift):
    rows, width = features.shape
    kinds, _, hidden = rel_weight.shape
    block = tile_values.shape[-1]
    nblocks = rows // block
    groups = lax.axis_size("grp")
    doms = lax.axis_size("dom")
    rels = lax.axis_size("rel")
    slots = doms * rels
    sources = nblocks + doms
    chunks = width // F_CHUNK
    columns = hidden // COL_PARTS
    anywhere = pl.BlockSpec(memory_space=pltpu.HBM)
    dma = pltpu.SemaphoreType.DMA
    return pl.pallas_call(
        functools.partial(kernel, groups, doms, rels),
        out_shape=jax.ShapeDtypeStruct((rows, hidden), jnp.bfloat16),
        in_specs=[anywhere] * 8,
        out_specs=pl.BlockSpec(memory_space=pltpu.VMEM),
        scratch_shapes=[
            pltpu.SMEM((1, doms), jnp.int32),
            pltpu.SMEM(tile_meta.shape, jnp.int32),
            pltpu.VMEM((1, hidden), jnp.float32),
            pltpu.VMEM((1, hidden), jnp.float32),
            pltpu.VMEM((sources * block, width), jnp.bfloat16),
            pltpu.VMEM((doms - 1, block, width), jnp.bfloat16),
            pltpu.VMEM((slots, block + CODE_ROWS, block), jnp.bfloat16),
            pltpu.VMEM((slots, block + CODE_ROWS, block), jnp.bfloat16),
            pltpu.VMEM((kinds * rows, sources * block), jnp.bfloat16),
            pltpu.VMEM((rows, kinds * F_CHUNK), jnp.bfloat16),
            pltpu.VMEM((chunks, kinds * F_CHUNK, hidden), jnp.bfloat16),
            pltpu.VMEM((width, hidden), jnp.bfloat16),
            pltpu.VMEM((rows, hidden), jnp.float32),
            pltpu.VMEM((COL_PARTS, slots, 2, columns), jnp.float32),
            pltpu.VMEM((COL_PARTS, groups, 2, columns), jnp.float32),
            pltpu.VMEM((rows, width), jnp.bfloat16),
            dma((4,)),
            dma(()),
            dma(()),
            dma((slots,)),
            dma((chunks, kinds)),
            dma(()),
            dma((slots,)),
            dma((slots,)),
            dma((chunks, doms - 1)),
            dma((chunks, doms - 1)),
            dma((COL_PARTS, slots)),
            dma((COL_PARTS, slots)),
            dma((COL_PARTS, groups)),
            dma((COL_PARTS, groups)),
        ],
        compiler_params=pltpu.CompilerParams(
            collective_id=0, has_side_effects=True, vmem_limit_bytes=62 * 1024 * 1024
        ),
        cost_estimate=pl.CostEstimate(
            flops=2 * rows * (kinds + 1) * width * hidden,
            bytes_accessed=2 * (kinds + 1) * width * hidden,
            transcendentals=rows * hidden,
        ),
    )(
        features,
        send_list.reshape(1, doms),
        tile_values,
        tile_meta,
        rel_weight,
        self_weight,
        bn_gain.reshape(1, hidden),
        bn_shift.reshape(1, hidden),
    )


def solution(mesh):
    return jax.shard_map(
        body,
        mesh=mesh,
        in_specs=(
            P(("grp", "dom", "rel"), None),
            P(("grp", "dom", "rel"), None, None),
            P(("grp", "dom", "rel"), None, None, None, None),
            P(("grp", "dom", "rel"), None, None, None),
            P(),
            P(),
            P(),
            P(),
        ),
        out_specs=P(("grp", "dom", "rel"), None),
        check_vma=False,
    )
```

```python
import functools

import jax
import jax.numpy as jnp
from jax import lax
from jax.experimental import pallas as pl
from jax.experimental.pallas import tpu as pltpu
from jax.sharding import PartitionSpec as P

MESH = pl.DeviceIdType.MESH
CODE_ROWS = 16
F_CHUNK = 256
COL_PARTS = 1
ROW_PARTS = 4


def repeat(count, body, static):
    if static:
        for index in range(count):
            body(index)
    else:

        @pl.loop(0, count)
        def _(index):
            body(index)


def aligned(index, size):
    return pl.ds(pl.multiple_of(index * size, size), size)


def kernel(
    groups,
    doms,
    rels,
    features,
    send_list_hbm,
    tile_values,
    tile_meta_hbm,
    rel_weight,
    self_weight,
    bn_gain_hbm,
    bn_shift_hbm,
    out,
    send_list,
    tile_meta,
    bn_gain,
    bn_shift,
    table,
    picked,
    message_out,
    message_in,
    adjacency,
    aggregated,
    weights,
    root,
    pre,
    group_stats,
    all_stats,
    own,
    result,
    out_sem,
    small_sem,
    own_sem,
    feature_sem,
    tile_sem,
    weight_sem,
    root_sem,
    message_send,
    message_recv,
    block_send,
    block_recv,
    group_send,
    group_recv,
    all_send,
    all_recv,
):
    rows, width = features.shape
    kinds, _, hidden = rel_weight.shape
    block = tile_values.shape[-1]
    nblocks = rows // block
    slots = doms * rels
    sources = nblocks + doms
    chunks = width // F_CHUNK
    columns = hidden // COL_PARTS
    static = slots <= 16
    my_grp = lax.axis_index("grp")
    my_dom = lax.axis_index("dom")
    my_rel = lax.axis_index("rel")
    me = my_dom * rels + my_rel

    def peer(offset):
        target = lax.rem(me + offset, slots)
        return target // rels, lax.rem(target, rels)

    def group_peer(offset):
        dom, rel = peer(offset)
        return {"dom": dom, "rel": rel}

    def far_peer(offset):
        return {"grp": lax.rem(my_grp + offset, groups)}

    def tile_copy(offset):
        dom, rel = peer(offset)
        return pltpu.make_async_copy(
            tile_values.at[0, dom, rel],
            message_out.at[offset, pl.ds(0, block)],
            tile_sem.at[offset],
        )

    own_tile = pltpu.make_async_copy(
        tile_values.at[0, my_dom, my_rel], message_in.at[0, pl.ds(0, block)], tile_sem.at[0]
    )
    own_features = pltpu.make_async_copy(features, table.at[pl.ds(0, rows)], feature_sem)

    small_copies = [
        pltpu.make_async_copy(source, target, small_sem.at[index])
        for index, (source, target) in enumerate(
            (
                (send_list_hbm, send_list),
                (tile_meta_hbm, tile_meta),
                (bn_gain_hbm, bn_gain),
                (bn_shift_hbm, bn_shift),
            )
        )
    ]
    for copy in small_copies:
        copy.start()
    own_copy = pltpu.make_async_copy(features, own, own_sem)
    own_copy.start()
    own_features.start()
    repeat(slots - 1, lambda i: tile_copy(i + 1).start(), static)
    own_tile.start()

    barrier = pltpu.get_barrier_semaphore()

    def greet_group(i):
        pl.semaphore_signal(barrier, inc=1, device_id=group_peer(i + 1), device_id_type=MESH)

    def greet_far(i):
        pl.semaphore_signal(barrier, inc=1, device_id=far_peer(i + 1), device_id_type=MESH)

    repeat(slots - 1, greet_group, static)
    repeat(groups - 1, greet_far, static)

    root_copy = pltpu.make_async_copy(self_weight, root, root_sem)
    root_copy.start()

    def weight_copy(chunk, kind):
        return pltpu.make_async_copy(
            rel_weight.at[kind, pl.ds(chunk * F_CHUNK, F_CHUNK)],
            weights.at[chunk, pl.ds(kind * F_CHUNK, F_CHUNK)],
            weight_sem.at[chunk, kind],
        )

    for chunk in range(chunks):
        for kind in range(kinds):
            weight_copy(chunk, kind).start()

    def write_code(offset, ref):
        dom, rel = peer(offset)
        source = tile_meta[0, dom, rel, 2]
        around = dom - (source - nblocks)
        around = jnp.where(around < 0, around + doms, around)
        place = jnp.where(source < nblocks, source, nblocks + around)
        row = tile_meta[0, dom, rel, 0] * nblocks + tile_meta[0, dom, rel, 1]
        code = jnp.where(tile_meta[0, dom, rel, 3] != 0, row * sources + place, -1)
        splat = jnp.full((CODE_ROWS, block), code.astype(jnp.float32), jnp.float32)
        ref[offset, pl.ds(block, CODE_ROWS), :] = splat.astype(jnp.bfloat16)

    for copy in small_copies:
        copy.wait()
    write_code(0, message_in)
    repeat(slots - 1, lambda i: write_code(i + 1, message_out), static)

    own_copy.wait()

    def pick(offset):
        chosen = send_list[0, lax.rem(my_dom + offset, doms)]
        chosen = jnp.full((block, width), chosen.astype(jnp.float32)).astype(jnp.bfloat16)
        total = own[pl.ds(0, block), :]
        for index in range(1, nblocks):
            here = own[pl.ds(index * block, block), :]
            total = jnp.where(chosen == jnp.bfloat16(index), here, total)
        return total

    for offset in range(1, doms):
        picked[offset - 1] = pick(offset)
    table[pl.ds(nblocks * block, block), :] = pick(0)

    pl.semaphore_wait(barrier, slots - 1 + groups - 1)

    def message_copy(offset):
        return pltpu.make_async_remote_copy(
            src_ref=message_out.at[offset],
            dst_ref=message_in.at[offset],
            send_sem=message_send.at[offset],
            recv_sem=message_recv.at[offset],
            device_id=group_peer(offset),
            device_id_type=MESH,
        )

    def send_message(i):
        tile_copy(i + 1).wait()
        message_copy(i + 1).start()

    repeat(slots - 1, send_message, static)

    def block_copy(offset, chunk):
        part = pl.ds(chunk * F_CHUNK, F_CHUNK)
        return pltpu.make_async_remote_copy(
            src_ref=picked.at[offset - 1, :, part],
            dst_ref=table.at[pl.ds((nblocks + offset) * block, block), part],
            send_sem=block_send.at[chunk, offset - 1],
            recv_sem=block_recv.at[chunk, offset - 1],
            device_id={"dom": lax.rem(my_dom + offset, doms)},
            device_id_type=MESH,
        )

    for chunk in range(chunks):
        for offset in range(1, doms):
            block_copy(offset, chunk).start()

    root_copy.wait()
    own_features.wait()
    pre[...] = jnp.dot(own[...], root[...], preferred_element_type=jnp.float32)

    own_tile.wait()
    repeat(slots - 1, lambda i: message_copy(i + 1).wait_recv(), static)

    zero = jnp.zeros((CODE_ROWS, block), jnp.bfloat16)

    def place_tile(row, source, strip):
        code = row * sources + source
        if static:
            total = zero
            wanted = jnp.bfloat16(code)
            for slot in range(slots):
                same = message_in[slot, pl.ds(block, CODE_ROWS), :] == wanted
                total = jnp.where(
                    same, message_in[slot, aligned(strip, CODE_ROWS), :], total
                )
        else:
            wanted = jnp.full((CODE_ROWS, block), code.astype(jnp.float32)).astype(jnp.bfloat16)

            def step(slot, total):
                same = message_in[slot, pl.ds(block, CODE_ROWS), :] == wanted
                return jnp.where(
                    same, message_in[slot, aligned(strip, CODE_ROWS), :], total
                )

            total = lax.fori_loop(0, slots, step, zero)
        first = pl.multiple_of(row * block + strip * CODE_ROWS, CODE_ROWS)
        adjacency[pl.ds(first, CODE_ROWS), aligned(source, block)] = total

    @pl.loop(0, block // CODE_ROWS)
    def _(strip):
        repeat(
            kinds * nblocks,
            lambda row: repeat(sources, lambda source: place_tile(row, source, strip), static),
            static,
        )

    def aggregate(chunk):
        for offset in range(1, doms):
            block_copy(offset, chunk).wait_recv()
        part = pl.ds(chunk * F_CHUNK, F_CHUNK)
        for kind in range(kinds):
            weight_copy(chunk, kind).wait()
        for kind in range(kinds):
            aggregated[:, pl.ds(kind * F_CHUNK, F_CHUNK)] = jnp.dot(
                adjacency[pl.ds(kind * rows, rows), :],
                table[:, part],
                preferred_element_type=jnp.float32,
            ).astype(jnp.bfloat16)

    for chunk in range(chunks - 1):
        aggregate(chunk)
        pre[...] += jnp.dot(
            aggregated[...], weights[chunk], preferred_element_type=jnp.float32
        )

    aggregate(chunks - 1)

    def group_copy(part, offset):
        return pltpu.make_async_remote_copy(
            src_ref=group_stats.at[part, 0],
            dst_ref=group_stats.at[part, offset],
            send_sem=group_send.at[part, offset],
            recv_sem=group_recv.at[part, offset],
            device_id=group_peer(offset),
            device_id_type=MESH,
        )

    def far_copy(part, offset):
        return pltpu.make_async_remote_copy(
            src_ref=all_stats.at[part, 0],
            dst_ref=all_stats.at[part, offset],
            send_sem=all_send.at[part, offset],
            recv_sem=all_recv.at[part, offset],
            device_id=far_peer(offset),
            device_id_type=MESH,
        )

    def combine(stats, part, count, each):
        entries = [stats[part, index] for index in range(count)]
        mean = sum(entry[0:1] for entry in entries) * (1.0 / count)
        spread = sum(entry[1:2] for entry in entries)
        apart = [entry[0:1] - mean for entry in entries]
        return mean, spread + sum(gap * gap for gap in apart) * each

    for part in range(COL_PARTS):
        span = pl.ds(part * columns, columns)
        value = pre[:, span] + jnp.dot(
            aggregated[...], weights[chunks - 1, :, span], preferred_element_type=jnp.float32
        )
        pre[:, span] = value
        mean = jnp.sum(value, axis=0, keepdims=True) * (1.0 / rows)
        centered = value - mean
        group_stats[part, 0, 0:1, :] = mean
        group_stats[part, 0, 1:2, :] = jnp.sum(centered * centered, axis=0, keepdims=True)
        repeat(slots - 1, lambda i: group_copy(part, i + 1).start(), static)

    for part in range(COL_PARTS):
        repeat(slots - 1, lambda i: group_copy(part, i + 1).wait_recv(), static)
        mean, spread = combine(group_stats, part, slots, float(rows))
        all_stats[part, 0, 0:1, :] = mean
        all_stats[part, 0, 1:2, :] = spread
        repeat(groups - 1, lambda i: far_copy(part, i + 1).start(), static)

    copies = []
    for part in range(COL_PARTS):
        span = pl.ds(part * columns, columns)
        repeat(groups - 1, lambda i: far_copy(part, i + 1).wait_recv(), static)
        mean, spread = combine(all_stats, part, groups, float(rows * slots))
        variance = spread * (1.0 / (rows * slots * groups))
        scale = bn_gain[:, span] / jnp.sqrt(variance + 1e-05)
        for quarter in range(ROW_PARTS):
            strip = pl.ds(quarter * (rows // ROW_PARTS), rows // ROW_PARTS)
            normed = (pre[strip, span] - mean) * scale + bn_shift[:, span]
            below = jnp.exp(jnp.minimum(normed, 0.0)) - 1.0
            result[strip, span] = jnp.where(normed > 0, normed, below).astype(jnp.bfloat16)
            copy = pltpu.make_async_copy(
                result.at[strip, span], out.at[strip, span], out_sem.at[part, quarter]
            )
            copy.start()
            copies.append(copy)

    repeat(slots - 1, lambda i: message_copy(i + 1).wait_send(), static)
    for chunk in range(chunks):
        for offset in range(1, doms):
            block_copy(offset, chunk).wait_send()
    for part in range(COL_PARTS):
        repeat(slots - 1, lambda i: group_copy(part, i + 1).wait_send(), static)
        repeat(groups - 1, lambda i: far_copy(part, i + 1).wait_send(), static)
    for copy in copies:
        copy.wait()


def body(features, send_list, tile_values, tile_meta, rel_weight, self_weight, bn_gain, bn_shift):
    rows, width = features.shape
    kinds, _, hidden = rel_weight.shape
    block = tile_values.shape[-1]
    nblocks = rows // block
    groups = lax.axis_size("grp")
    doms = lax.axis_size("dom")
    rels = lax.axis_size("rel")
    slots = doms * rels
    sources = nblocks + doms
    chunks = width // F_CHUNK
    columns = hidden // COL_PARTS
    anywhere = pl.BlockSpec(memory_space=pltpu.HBM)
    dma = pltpu.SemaphoreType.DMA
    return pl.pallas_call(
        functools.partial(kernel, groups, doms, rels),
        out_shape=jax.ShapeDtypeStruct((rows, hidden), jnp.bfloat16),
        in_specs=[anywhere] * 8,
        out_specs=anywhere,
        scratch_shapes=[
            pltpu.SMEM((1, doms), jnp.int32),
            pltpu.SMEM(tile_meta.shape, jnp.int32),
            pltpu.VMEM((1, hidden), jnp.float32),
            pltpu.VMEM((1, hidden), jnp.float32),
            pltpu.VMEM((sources * block, width), jnp.bfloat16),
            pltpu.VMEM((doms - 1, block, width), jnp.bfloat16),
            pltpu.VMEM((slots, block + CODE_ROWS, block), jnp.bfloat16),
            pltpu.VMEM((slots, block + CODE_ROWS, block), jnp.bfloat16),
            pltpu.VMEM((kinds * rows, sources * block), jnp.bfloat16),
            pltpu.VMEM((rows, kinds * F_CHUNK), jnp.bfloat16),
            pltpu.VMEM((chunks, kinds * F_CHUNK, hidden), jnp.bfloat16),
            pltpu.VMEM((width, hidden), jnp.bfloat16),
            pltpu.VMEM((rows, hidden), jnp.float32),
            pltpu.VMEM((COL_PARTS, slots, 2, columns), jnp.float32),
            pltpu.VMEM((COL_PARTS, groups, 2, columns), jnp.float32),
            pltpu.VMEM((rows, width), jnp.bfloat16),
            pltpu.VMEM((rows, hidden), jnp.bfloat16),
            dma((COL_PARTS, ROW_PARTS)),
            dma((4,)),
            dma(()),
            dma(()),
            dma((slots,)),
            dma((chunks, kinds)),
            dma(()),
            dma((slots,)),
            dma((slots,)),
            dma((chunks, doms - 1)),
            dma((chunks, doms - 1)),
            dma((COL_PARTS, slots)),
            dma((COL_PARTS, slots)),
            dma((COL_PARTS, groups)),
            dma((COL_PARTS, groups)),
        ],
        compiler_params=pltpu.CompilerParams(
            collective_id=0, has_side_effects=True, vmem_limit_bytes=62 * 1024 * 1024
        ),
        cost_estimate=pl.CostEstimate(
            flops=2 * rows * (kinds + 1) * width * hidden,
            bytes_accessed=2 * (kinds + 1) * width * hidden,
            transcendentals=rows * hidden,
        ),
    )(
        features,
        send_list.reshape(1, doms),
        tile_values,
        tile_meta,
        rel_weight,
        self_weight,
        bn_gain.reshape(1, hidden),
        bn_shift.reshape(1, hidden),
    )


def solution(mesh):
    return jax.shard_map(
        body,
        mesh=mesh,
        in_specs=(
            P(("grp", "dom", "rel"), None),
            P(("grp", "dom", "rel"), None, None),
            P(("grp", "dom", "rel"), None, None, None, None),
            P(("grp", "dom", "rel"), None, None, None),
            P(),
            P(),
            P(),
            P(),
        ),
        out_specs=P(("grp", "dom", "rel"), None),
        check_vma=False,
    )
```
